32 devices in a mesh: replica: 8 (over y, x, core), fsdp: 4 (over z).
Axes of the slice: x: 2, y: 2, z: 4, core: 2. Of those that a mesh axis runs over, the one named last changes fastest.
Arguments:
- tokens: bfloat16 [4096, 8192], P(('replica', 'fsdp')), may hold values from -6 to 6
- weight: bfloat16 [192, 8192], P(None, 'fsdp'), may hold values from -0.0625 to 0.0625
- cotangent: bfloat16 [4096, 192], P(('replica', 'fsdp')), may hold values from -0.119628906 to 0.119628906
- momentum: float32 [8, 192, 8192], P('replica', None, 'fsdp'), may hold values from -6 to 6
- chosen: int32 [8, 3, 128, 32], P('replica', None, 'fsdp'), may hold values from 0 to 4095, as said below
Outputs:
- new_momentum: float32 [8, 192, 8192], P('replica', None, 'fsdp')
- update: float32 [192, 8192], P(None, 'fsdp')
The draws below stay inside these ranges and needn't reach their ends.
Inputs may be any that keep to these rules, and one draw needn't show every extreme that they name: `chosen`: within each block the 32 positions are distinct; the block's 64 * 64 positions fall into 32 equal runs of consecutive positions and each run holds exactly one of them.
All inputs are finite; a program needn't handle non-finite values.
Results may differ from the reference program's by a relative error of at most 0.003.
Values may be sent and summed in bfloat16 or wider, within the bound.
A program may use at most 64 MiB of HBM per device.

```python
import math
import jax
import jax.numpy as jnp
from jax import lax

D = 8192
HID = 192
SPAN = 64
TOPK = 32
TOK_DEV = 128
TOKENS = 4096
N_REPLICA = 8
N_FSDP = 4


def draw_chosen(key, part):
    key = jax.random.fold_in(key, 7)
    run_length = SPAN * SPAN // TOPK
    layout = (N_REPLICA, HID // SPAN, D // SPAN, TOPK)
    jitter = jax.random.randint(key, layout, 0, run_length, dtype=jnp.int32)
    run_starts = jnp.arange(TOPK, dtype=jnp.int32) * run_length
    return (run_starts + jitter).astype(jnp.int32)


def block_scale(own_key, dims, shards, low, top_value):
    level, own = 1.0, jax.random.fold_in(own_key, 6)
    for dim, blocks in shards:
        steps = jnp.exp(jax.random.uniform(jax.random.fold_in(own, dim), (blocks,), jnp.float32, low / len(shards), top_value / len(shards)))
        level = level * jnp.repeat(steps, dims[dim] // blocks).reshape([-1 if axis == dim else 1 for axis in range(len(dims))])
    return level


def noise(key, extent, deviation, reach, pieces=(), kind=jnp.bfloat16):
    array = jax.random.normal(key, extent, jnp.float32) * deviation
    if len(pieces) > 0:
        array = block_scale(key, extent, pieces, -0.22, 0.18) * array
    return jnp.clip(array, min=-reach, max=reach).astype(kind)


def setup_inputs(seed: int = 0) -> dict:
    seeds = jax.random.split(jax.random.key(seed), 6)
    return {
        "tokens": noise(seeds[0], (TOKENS, D), 1.0, 6.0, ((0, 32),)),
        "weight": noise(seeds[1], (HID, D), D ** -0.5, 0.0625, ((1, 4),)),
        "cotangent": noise(seeds[2], (TOKENS, HID), 0.02, 0.119628906, ((0, 32),)),
        "momentum": noise(seeds[3], (N_REPLICA, HID, D), 1.0, 6.0, ((0, 8), (2, 4)), jnp.float32),
        "chosen": draw_chosen(jax.random.fold_in(seeds[5], 71), 0),
    }


decay = 0.999

def cosine_table():
    points = jnp.arange(SPAN, dtype=jnp.float32)
    angles = math.pi * (2.0 * points[None, :] + 1.0) * points[:, None] / (2.0 * SPAN)
    scales = jnp.where(points[:, None] == 0, math.sqrt(1.0 / SPAN), math.sqrt(2.0 / SPAN))
    return (scales * jnp.cos(angles)).astype(jnp.float32)

def forward_dct(moment, cosines):
    blocks_a = moment.shape[0] // SPAN
    blocks_b = moment.shape[1] // SPAN
    tiles = moment.reshape(blocks_a, SPAN, blocks_b, SPAN)
    coefficients = jnp.einsum('ki,aibj,lj->abkl', cosines, tiles, cosines, precision=lax.Precision.HIGHEST)
    return coefficients.reshape(blocks_a, blocks_b, SPAN * SPAN)

def inverse_dct(spread, cosines):
    blocks_a = spread.shape[0]
    blocks_b = spread.shape[1]
    tiles = spread.reshape(blocks_a, blocks_b, SPAN, SPAN)
    moment = jnp.einsum('ki,abkl,lj->aibj', cosines, tiles, cosines, precision=lax.Precision.HIGHEST)
    return moment.reshape(blocks_a * SPAN, blocks_b * SPAN)

def place_values(values, positions, blocks_a, blocks_b):
    row_blocks = jnp.arange(blocks_a, dtype=jnp.int32)[:, None, None]
    col_blocks = jnp.arange(blocks_b, dtype=jnp.int32)[None, :, None]
    spread = jnp.zeros((blocks_a, blocks_b, SPAN * SPAN), values.dtype)
    return spread.at[row_blocks, col_blocks, positions].add(values)

def replica_step(activations, upstream, weight, moment, positions, cosines):
    preact = jnp.dot(activations, weight.T, preferred_element_type=jnp.float32)
    sigmoid_value = jax.nn.sigmoid(preact)
    gate_grad = (upstream.astype(jnp.float32) * sigmoid_value * (1.0 + preact * (1.0 - sigmoid_value))).astype(jnp.bfloat16)
    sources = activations.reshape(N_FSDP, TOK_DEV, D).astype(jnp.float32)
    grads = gate_grad.reshape(N_FSDP, TOK_DEV, HID).astype(jnp.float32)
    per_source = jnp.einsum('fth,ftd->fhd', grads, sources)
    rounded = lax.optimization_barrier(per_source.astype(jnp.bfloat16))
    gradient = lax.optimization_barrier(jnp.sum(rounded.astype(jnp.float32), axis=0))
    moment = decay * moment + gradient
    coefficients = forward_dct(moment, cosines)
    picked = jnp.take_along_axis(coefficients, positions, axis=2)
    own = place_values(picked, positions, HID // SPAN, D // SPAN)
    return (moment - inverse_dct(own, cosines), picked)

def reference(tokens, weight, cotangent, momentum, chosen):
    cosines = cosine_table()
    acts = tokens.reshape(N_REPLICA, N_FSDP * TOK_DEV, D)
    upstreams = cotangent.reshape(N_REPLICA, N_FSDP * TOK_DEV, HID)

    def one_replica(members):
        return replica_step(members[0], members[1], weight, members[2], members[3], cosines)
    new_momentum, picked = lax.map(one_replica, (acts, upstreams, momentum, chosen))
    spread = place_values(picked, chosen, HID // SPAN, D // SPAN)
    update = inverse_dct(spread, cosines)
    return (new_momentum, update)
```

```python
import functools
import math

import jax
import jax.numpy as jnp
import ml_dtypes
import numpy as np
from jax import lax
from jax.experimental import pallas as pl
from jax.experimental.pallas import tpu as pltpu
from jax.sharding import PartitionSpec as P

SPAN = 64
TOPK = 32
RUN = SPAN * SPAN // TOPK
CHUNK = 512
GROUP = 8
decay = 0.999

BF = jnp.bfloat16
F32 = jnp.float32
MESH = pl.DeviceIdType.MESH


def cosine_table():
    n = np.arange(SPAN, dtype=np.float64)
    angles = math.pi * (2.0 * n[None, :] + 1.0) * n[:, None] / (2.0 * SPAN)
    scales = np.where(n[:, None] == 0, math.sqrt(1.0 / SPAN), math.sqrt(2.0 / SPAN))
    return (scales * np.cos(angles)).astype(np.float32)


def halves(table):
    high = table.astype(ml_dtypes.bfloat16)
    low = (table - high.astype(np.float32)).astype(ml_dtypes.bfloat16)
    return high, low


def split(x):
    high = x.astype(BF)
    return high, (x - high.astype(F32)).astype(BF)


def mm(a, b):
    return jnp.dot(a, b, preferred_element_type=F32)


def mm_nt(a, b):
    return lax.dot_general(a, b, (((1,), (1,)), ((), ())), preferred_element_type=F32)


def transform(x, left_high, left_low, right_high, right_low):
    high, low = split(x)
    half = mm(left_high, high) + mm(left_high, low) + mm(left_low, high)
    width = right_high.shape[0]
    parts = []
    for start in range(0, x.shape[1], width):
        high, low = split(half[:, start : start + width])
        parts.append(mm(high, right_high) + mm(high, right_low) + mm(low, right_high))
    return jnp.concatenate(parts, axis=1)


def kernel(
    nf, nr,
    tok, weight, cot, mom, chosen,
    fwd_lh, fwd_ll, fwd_rh, fwd_rl, inv_lh, inv_ll, inv_rh, inv_rl, eye, pair, wide, spot, wide8,
    new_out, upd_out,
    tok_v, w_own, wall, cot_v, mom_v, xall, gt, pos, delta, vt, new_v, upd_v,
    s1_s, s1_r, s2_s, s2_r, s3_s, s3_r, x_s, x_r, g_s, g_r, p_s, p_r, v_s, v_r, loc, xloc, osem,
):
    r, f = lax.axis_index("replica"), lax.axis_index("fsdp")
    rows, dc = weight.shape
    td = tok.shape[0]
    nch = dc // CHUNK
    half = dc // 2
    inner = lax.rem(r, 8)
    base = r - inner
    quad, side = inner // 2, lax.rem(inner, 2)
    piece = rows // 4

    def fpeer(k):
        return lax.rem(f + k, nf)

    def fsource(k):
        return lax.rem(f + nf - k, nf)

    def remote(src, dst, send, recv, to_r, to_f):
        return pltpu.make_async_remote_copy(
            src_ref=src, dst_ref=dst, send_sem=send, recv_sem=recv,
            device_id=(to_r, to_f), device_id_type=MESH,
        )

    c_tok = pltpu.make_async_copy(tok, tok_v, loc.at[0])
    c_w = pltpu.make_async_copy(weight, w_own, loc.at[1])
    c_cot = pltpu.make_async_copy(cot, cot_v, loc.at[2])
    c_mom = pltpu.make_async_copy(mom.at[0], mom_v, loc.at[3])
    c_pos = pltpu.make_async_copy(chosen.at[0], pos.at[r], loc.at[4])
    c_x = [
        pltpu.make_async_copy(
            tok.at[:, pl.ds(pl.multiple_of(f * dc + c * CHUNK, CHUNK), CHUNK)],
            xall.at[c, pl.ds(pl.multiple_of(f * td, td), td)],
            xloc.at[c],
        )
        for c in range(nch)
    ]
    for copy in [c_w, c_tok, c_pos, c_cot, c_mom] + c_x:
        copy.start()

    barrier = pltpu.get_barrier_semaphore()
    for k in range(1, nf):
        pl.semaphore_signal(barrier, inc=1, device_id=(r, fpeer(k)), device_id_type=MESH)
    for t in range(1, nr):
        pl.semaphore_signal(
            barrier, inc=1, device_id=(lax.rem(r + t, nr), f), device_id_type=MESH
        )
    pl.semaphore_wait(barrier, nf - 1 + nr - 1)

    own_rows = pl.ds(pl.multiple_of(quad * piece, 16), piece)
    stage1 = {}
    for k in range(1, nf):
        stage1[k] = remote(
            weight.at[own_rows, pl.ds(pl.multiple_of(side * half, half), half)],
            wall.at[f, side, own_rows],
            s1_s.at[k], s1_r.at[k], r, fpeer(k),
        )
        stage1[k].start()
    sent_pos = {}
    for t in range(1, nr):
        sent_pos[t] = remote(
            chosen.at[0], pos.at[r], p_s.at[t], p_r.at[t], lax.rem(r + t, nr), f
        )
        sent_pos[t].start()

    xs = {}

    def send_x(c):
        for k in range(1, nf):
            to = fpeer(k)
            xs[c, k] = remote(
                tok.at[:, pl.ds(pl.multiple_of(to * dc + c * CHUNK, CHUNK), CHUNK)],
                xall.at[c, pl.ds(pl.multiple_of(f * td, td), td)],
                x_s.at[k, c], x_r.at[k, c], r, to,
            )
            xs[c, k].start()

    c_tok.wait()
    c_w.wait()
    pre = mm_nt(w_own[...], tok_v[:, pl.ds(pl.multiple_of(f * dc, CHUNK), dc)])

    for k in range(1, nf):
        stage1[k].wait_send()
    send_x(0)

    stage2 = {}
    for k in range(1, nf):
        stage1[k].wait_recv()
        for t in range(1, 4):
            block = wall.at[fsource(k), side, own_rows]
            stage2[k, t] = remote(
                block, block, s2_s.at[k, t], s2_r.at[k, t],
                base + lax.rem(quad + t, 4) * 2 + side, f,
            )
            stage2[k, t].start()
    if nch > 1:
        send_x(1)

    c_pos.wait()
    for t in range(1, nr):
        sent_pos[t].wait_recv()
    row = lax.broadcasted_iota(jnp.int32, (rows, CHUNK), 0)
    col = lax.broadcasted_iota(jnp.int32, (rows, CHUNK), 1)
    target = (lax.rem(row, 2) * SPAN + lax.rem(col, SPAN)).astype(F32)
    run_start = lax.broadcasted_iota(jnp.int32, pos.shape[2:], 1) * RUN

    def locate(i, carry):
        parts = []
        for a in range(rows // SPAN):
            offset = (pos[i, a] - run_start).astype(F32).astype(BF)
            parts.append(mm_nt(pair[...], offset))
        spots = jnp.concatenate(parts, axis=0).astype(BF)
        for c in range(nch):
            far = mm(spots, wide[:, c * CHUNK : (c + 1) * CHUNK])
            delta[c, i] = (far - target).astype(BF)
        return carry

    def locate_some(low, high):
        lax.fori_loop(low, high, locate, 0)

    locate_some(0, nr // 2)

    stage3 = {}
    for k in range(1, nf):
        for t in range(1, 4):
            stage2[k, t].wait_recv()
        block = wall.at[fsource(k), side]
        stage3[k] = remote(block, block, s3_s.at[k], s3_r.at[k], r + 1 - 2 * side, f)
        stage3[k].start()
    for k in range(1, nf):
        stage3[k].wait_recv()
        source = fsource(k)
        for h in range(2):
            cols = pl.ds(pl.multiple_of(source * dc + h * half, 128), half)
            pre = pre + mm_nt(wall[source, h], tok_v[:, cols])

    c_cot.wait()
    up = mm_nt(eye[...], cot_v[...])
    s = jax.nn.sigmoid(pre)
    mine = pl.ds(pl.multiple_of(f * td, td), td)
    gt[:, mine] = (up * s * (1.0 + pre * (1.0 - s))).astype(BF)
    sent_g = {}
    for k in range(1, nf):
        sent_g[k] = remote(
            gt.at[:, mine], gt.at[:, mine], g_s.at[k], g_r.at[k], r, fpeer(k)
        )
        sent_g[k].start()

    def wait_x_sent(c):
        for k in range(1, nf):
            xs[c, k].wait_send()

    for c in range(2, nch):
        if c == 2:
            wait_x_sent(0)
            send_x(c)
    locate_some(nr // 2, nr)
    for k in range(1, nf):
        sent_g[k].wait_recv()
    c_mom.wait()

    sent_v = {}
    outs = []

    def first_half(c):
        c_x[c].wait()
        for k in range(1, nf):
            xs[c, k].wait_recv()
        cols = slice(c * CHUNK, (c + 1) * CHUNK)
        moment = decay * mom_v[:, cols] + mm(gt[...], xall[c])
        coef = transform(moment, fwd_lh[...], fwd_ll[...], fwd_rh[...], fwd_rl[...])
        own = jnp.where(delta[c, r].astype(F32) == 0.0, coef, 0.0)
        high, low = split(own)
        nbc = CHUNK // SPAN
        vt[c, r] = (mm_nt(spot[...], high) + mm_nt(spot[...], low))[:nbc]
        for t in range(1, nr):
            sent_v[c, t] = remote(
                vt.at[c, r], vt.at[c, r], v_s.at[c, t], v_r.at[c, t], lax.rem(r + t, nr), f
            )
            sent_v[c, t].start()
        new_v[:, cols] = moment - transform(
            own, inv_lh[...], inv_ll[...], inv_rh[...], inv_rl[...]
        )
        copy = pltpu.make_async_copy(new_v.at[:, cols], new_out.at[0, :, cols], osem.at[0, c])
        copy.start()
        outs.append(copy)

    def second_half(c):
        for t in range(1, nr):
            sent_v[c, t].wait_recv()
        cols = slice(c * CHUNK, (c + 1) * CHUNK)
        nbc = CHUNK // SPAN

        def add_group(g, total):
            first = pl.multiple_of(g * GROUP, GROUP)
            high, low = split(vt[c, pl.ds(first, GROUP)].reshape(GROUP * nbc, rows))
            both = mm_nt(eye[...], jnp.concatenate([high, low], axis=0)).astype(BF)
            for i in range(GROUP):
                value = mm(both, wide8[i])
                total = total + jnp.where(delta[c, first + i].astype(F32) == 0.0, value, 0.0)
            return total

        total = jnp.zeros((rows, CHUNK), F32)
        if nr == GROUP:
            total = add_group(0, total)
        else:
            total = lax.fori_loop(0, nr // GROUP, add_group, total)
        upd_v[:, cols] = transform(total, inv_lh[...], inv_ll[...], inv_rh[...], inv_rl[...])
        copy = pltpu.make_async_copy(upd_v.at[:, cols], upd_out.at[:, cols], osem.at[1, c])
        copy.start()
        outs.append(copy)

    for c in range(nch):
        first_half(c)
        if c + 3 < nch:
            wait_x_sent(c + 1)
            send_x(c + 3)
        if c > 0:
            second_half(c - 1)
    second_half(nch - 1)

    for c in range(max(nch - 2, 0), nch):
        wait_x_sent(c)
    for k in range(1, nf):
        for t in range(1, 4):
            stage2[k, t].wait_send()
        stage3[k].wait_send()
        sent_g[k].wait_send()
    for t in range(1, nr):
        sent_pos[t].wait_send()
        for c in range(nch):
            sent_v[c, t].wait_send()
    for copy in outs:
        copy.wait()


def shards(nf, nr, tokens, weight, cotangent, momentum, chosen):
    td = tokens.shape[0]
    rows, dc = weight.shape
    nb = dc // SPAN
    nch = dc // CHUNK
    nbc = CHUNK // SPAN
    table = cosine_table()
    left = np.kron(np.eye(rows // SPAN, dtype=np.float32), table)
    right = np.kron(np.eye(4, dtype=np.float32), table)
    fwd_lh, fwd_ll = halves(left)
    fwd_rh, fwd_rl = halves(np.ascontiguousarray(right.T))
    inv_lh, inv_ll = halves(np.ascontiguousarray(left.T))
    inv_rh, inv_rl = halves(right)
    bf = ml_dtypes.bfloat16
    eye = np.eye(rows, dtype=np.float32).astype(bf)
    pair = (np.arange(SPAN)[:, None] // 2 == np.arange(TOPK)[None, :]).astype(bf)
    wide = (np.arange(dc)[None, :] // SPAN == np.arange(nb)[:, None]).astype(bf)
    spot = (np.arange(CHUNK)[None, :] // SPAN == np.arange(2 * nbc)[:, None]).astype(bf)
    slot = np.arange(2 * GROUP * nbc) % (GROUP * nbc)
    wide8 = (
        (slot[None, :, None] // nbc == np.arange(GROUP)[:, None, None])
        & (slot[None, :, None] % nbc == np.arange(CHUNK)[None, None, :] // SPAN)
    ).astype(bf)
    consts = (
        fwd_lh, fwd_ll, fwd_rh, fwd_rl, inv_lh, inv_ll, inv_rh, inv_rl, eye, pair, wide, spot, wide8
    )
    dma = pltpu.SemaphoreType.DMA
    vm = pltpu.VMEM
    new, update = pl.pallas_call(
        functools.partial(kernel, nf, nr),
        out_shape=(
            jax.ShapeDtypeStruct((1, rows, dc), F32),
            jax.ShapeDtypeStruct((rows, dc), F32),
        ),
        in_specs=[pl.BlockSpec(memory_space=pl.ANY)] * 5
        + [pl.BlockSpec(memory_space=pltpu.VMEM)] * len(consts),
        out_specs=(pl.BlockSpec(memory_space=pl.ANY), pl.BlockSpec(memory_space=pl.ANY)),
        scratch_shapes=[
            vm(tokens.shape, BF),
            vm(weight.shape, BF),
            vm((nf, 2, rows, dc // 2), BF),
            vm(cotangent.shape, BF),
            vm((rows, dc), F32),
            vm((nch, nf * td, CHUNK), BF),
            vm((rows, nf * td), BF),
            vm((nr,) + chosen.shape[1:], jnp.int32),
            vm((nch, nr, rows, CHUNK), BF),
            vm((nch, nr, nbc, rows), F32),
            vm((rows, dc), F32),
            vm((rows, dc), F32),
            dma((nf,)), dma((nf,)),
            dma((nf, 4)), dma((nf, 4)),
            dma((nf,)), dma((nf,)),
            dma((nf, nch)), dma((nf, nch)),
            dma((nf,)), dma((nf,)),
            dma((nr,)), dma((nr,)),
            dma((nch, nr)), dma((nch, nr)),
            dma((5,)), dma((nch,)), dma((2, nch)),
        ],
        compiler_params=pltpu.CompilerParams(
            collective_id=0, has_side_effects=True, vmem_limit_bytes=48 * 1024 * 1024
        ),
    )(tokens, weight, cotangent, momentum, chosen, *consts)
    return new, update


def solution(mesh):
    return jax.shard_map(
        functools.partial(shards, mesh.shape["fsdp"], mesh.shape["replica"]),
        mesh=mesh,
        in_specs=(
            P(("replica", "fsdp"), None),
            P(None, "fsdp"),
            P(("replica", "fsdp"), None),
            P("replica", None, "fsdp"),
            P("replica", None, "fsdp", None),
        ),
        out_specs=(P("replica", None, "fsdp"), P(None, "fsdp")),
        check_vma=False,
    )
```

```python
import functools
import math

import jax
import jax.numpy as jnp
from jax import lax
from jax.experimental import pallas as pl
from jax.experimental.pallas import tpu as pltpu
from jax.sharding import PartitionSpec as P

SPAN = 64
TOPK = 32
RUN = SPAN * SPAN // TOPK
CHUNK = 512
GROUP = 8
decay = 0.999

BF = jnp.bfloat16
F32 = jnp.float32
MESH = pl.DeviceIdType.MESH


def iotas(shape):
    return (
        lax.broadcasted_iota(jnp.int32, shape, 0),
        lax.broadcasted_iota(jnp.int32, shape, 1),
    )


def cosine_blocks(size, transposed):
    row, col = iotas((size, size))
    same = (row // SPAN) == (col // SPAN)
    if transposed:
        row, col = col, row
    k, n = lax.rem(row, SPAN), lax.rem(col, SPAN)
    turn = lax.rem((2 * n + 1) * k, 4 * SPAN)
    turn = jnp.minimum(turn, 4 * SPAN - turn)
    flip = turn > SPAN
    turn = jnp.where(flip, 2 * SPAN - turn, turn)
    angle = turn.astype(F32) * (math.pi / (2 * SPAN))
    square = angle * angle
    series = jnp.full_like(square, 1.0 / math.factorial(12))
    for order in (10, 8, 6, 4, 2, 0):
        sign = 1.0 if order % 4 == 0 else -1.0
        series = series * square + sign / math.factorial(order)
    series = jnp.where(flip, -series, series)
    scale = jnp.where(k == 0, math.sqrt(1.0 / SPAN), math.sqrt(2.0 / SPAN))
    return split(jnp.where(same, scale * series, 0.0))


def split(x):
    high = x.astype(BF)
    return high, (x - high.astype(F32)).astype(BF)


def mm(a, b):
    return jnp.dot(a, b, preferred_element_type=F32)


def mm_nt(a, b):
    return lax.dot_general(a, b, (((1,), (1,)), ((), ())), preferred_element_type=F32)


def transform(x, left_high, left_low, right_high, right_low):
    high, low = split(x)
    half = mm(left_high, high) + mm(left_high, low) + mm(left_low, high)
    width = right_high.shape[0]
    parts = []
    for start in range(0, x.shape[1], width):
        high, low = split(half[:, start : start + width])
        parts.append(mm(high, right_high) + mm(high, right_low) + mm(low, right_high))
    return jnp.concatenate(parts, axis=1)


def kernel(
    nf, nr,
    tok, weight, cot, mom, chosen,
    new_out, upd_out,
    tok_v, w_own, wall, cot_v, mom_v, xall, gt, pos, delta, vt, new_v, upd_v,
    fwd_lh, fwd_ll, fwd_rh, fwd_rl, inv_lh, inv_ll, inv_rh, inv_rl, eye, spot, wide8,
    s1_s, s1_r, s2_s, s2_r, s3_s, s3_r, x_s, x_r, g_s, g_r, p_s, p_r, v_s, v_r, loc, xloc, osem,
):
    r, f = lax.axis_index("replica"), lax.axis_index("fsdp")
    rows, dc = weight.shape
    td = tok.shape[0]
    nch = dc // CHUNK
    half = dc // 2
    inner = lax.rem(r, 8)
    base = r - inner
    quad, side = inner // 2, lax.rem(inner, 2)
    piece = rows // 4

    def fpeer(k):
        return lax.rem(f + k, nf)

    def fsource(k):
        return lax.rem(f + nf - k, nf)

    def remote(src, dst, send, recv, to_r, to_f):
        return pltpu.make_async_remote_copy(
            src_ref=src, dst_ref=dst, send_sem=send, recv_sem=recv,
            device_id=(to_r, to_f), device_id_type=MESH,
        )

    c_tok = pltpu.make_async_copy(tok, tok_v, loc.at[0])
    c_w = pltpu.make_async_copy(weight, w_own, loc.at[1])
    c_cot = pltpu.make_async_copy(cot, cot_v, loc.at[2])
    c_mom = pltpu.make_async_copy(mom.at[0], mom_v, loc.at[3])
    c_pos = pltpu.make_async_copy(chosen.at[0], pos.at[r], loc.at[4])
    c_x = [
        pltpu.make_async_copy(
            tok.at[:, pl.ds(pl.multiple_of(f * dc + c * CHUNK, CHUNK), CHUNK)],
            xall.at[c, pl.ds(pl.multiple_of(f * td, td), td)],
            xloc.at[c],
        )
        for c in range(nch)
    ]
    for copy in [c_w, c_tok, c_pos, c_cot, c_mom] + c_x:
        copy.start()

    barrier = pltpu.get_barrier_semaphore()
    for k in range(1, nf):
        pl.semaphore_signal(barrier, inc=1, device_id=(r, fpeer(k)), device_id_type=MESH)
    for t in range(1, nr):
        pl.semaphore_signal(
            barrier, inc=1, device_id=(lax.rem(r + t, nr), f), device_id_type=MESH
        )
    pl.semaphore_wait(barrier, nf - 1 + nr - 1)

    own_rows = pl.ds(pl.multiple_of(quad * piece, 16), piece)
    stage1 = {}
    for k in range(1, nf):
        stage1[k] = remote(
            weight.at[own_rows, pl.ds(pl.multiple_of(side * half, half), half)],
            wall.at[f, side, own_rows],
            s1_s.at[k], s1_r.at[k], r, fpeer(k),
        )
        stage1[k].start()
    sent_pos = {}
    for t in range(1, nr):
        sent_pos[t] = remote(
            chosen.at[0], pos.at[r], p_s.at[t], p_r.at[t], lax.rem(r + t, nr), f
        )
        sent_pos[t].start()

    nbc = CHUNK // SPAN
    for high_ref, low_ref, size, transposed in (
        (fwd_lh, fwd_ll, rows, False),
        (fwd_rh, fwd_rl, fwd_rh.shape[0], True),
        (inv_lh, inv_ll, rows, True),
        (inv_rh, inv_rl, fwd_rh.shape[0], False),
    ):
        high_ref[...], low_ref[...] = cosine_blocks(size, transposed)

    def one_hot(equal):
        return jnp.where(equal, 1.0, 0.0).astype(BF)

    row, col = iotas((rows, rows))
    eye[...] = one_hot(row == col)
    row, col = iotas((2 * nbc, CHUNK))
    spot[...] = one_hot(row == col // SPAN)
    row, col = iotas((2 * GROUP * nbc, CHUNK))
    near = lax.rem(row, GROUP * nbc) - col // SPAN
    for i in range(GROUP):
        wide8[i] = one_hot(near == i * nbc)

    xs = {}

    def send_x(c):
        for k in range(1, nf):
            to = fpeer(k)
            xs[c, k] = remote(
                tok.at[:, pl.ds(pl.multiple_of(to * dc + c * CHUNK, CHUNK), CHUNK)],
                xall.at[c, pl.ds(pl.multiple_of(f * td, td), td)],
                x_s.at[k, c], x_r.at[k, c], r, to,
            )
            xs[c, k].start()

    c_tok.wait()
    c_w.wait()
    pre = mm_nt(w_own[...], tok_v[:, pl.ds(pl.multiple_of(f * dc, CHUNK), dc)])

    for k in range(1, nf):
        stage1[k].wait_send()
    send_x(0)

    stage2 = {}
    for k in range(1, nf):
        stage1[k].wait_recv()
        for t in range(1, 4):
            block = wall.at[fsource(k), side, own_rows]
            stage2[k, t] = remote(
                block, block, s2_s.at[k, t], s2_r.at[k, t],
                base + lax.rem(quad + t, 4) * 2 + side, f,
            )
            stage2[k, t].start()
    if nch > 1:
        send_x(1)

    c_pos.wait()
    for t in range(1, nr):
        sent_pos[t].wait_recv()
    row, col = iotas((rows, CHUNK))
    target = (lax.rem(row, 2) * SPAN + lax.rem(col, SPAN)).astype(F32)
    run_start = lax.broadcasted_iota(jnp.int32, pos.shape[2:], 1) * RUN

    row, col = iotas((SPAN, TOPK))
    pair = one_hot(row // 2 == col)
    row, col = iotas((dc // SPAN, CHUNK))
    near = row - col // SPAN

    def locate(i, carry):
        parts = []
        for a in range(rows // SPAN):
            offset = (pos[i, a] - run_start).astype(F32).astype(BF)
            parts.append(mm_nt(pair, offset))
        spots = jnp.concatenate(parts, axis=0).astype(BF)
        for c in range(nch):
            far = mm(spots, one_hot(near == c * nbc))
            delta[c, i] = (far - target).astype(BF)
        return carry

    def locate_some(low, high):
        lax.fori_loop(low, high, locate, 0)

    locate_some(0, nr // 2)

    stage3 = {}
    for k in range(1, nf):
        for t in range(1, 4):
            stage2[k, t].wait_recv()
        block = wall.at[fsource(k), side]
        stage3[k] = remote(block, block, s3_s.at[k], s3_r.at[k], r + 1 - 2 * side, f)
        stage3[k].start()
    for k in range(1, nf):
        stage3[k].wait_recv()
        source = fsource(k)
        for h in range(2):
            cols = pl.ds(pl.multiple_of(source * dc + h * half, 128), half)
            pre = pre + mm_nt(wall[source, h], tok_v[:, cols])

    c_cot.wait()
    up = cot_v[...].astype(F32)
    s = jax.nn.sigmoid(pre)
    mine = pl.ds(pl.multiple_of(f * td, td), td)
    gt[:, mine] = (up * s * (1.0 + pre * (1.0 - s))).astype(BF)
    sent_g = {}
    for k in range(1, nf):
        sent_g[k] = remote(
            gt.at[:, mine], gt.at[:, mine], g_s.at[k], g_r.at[k], r, fpeer(k)
        )
        sent_g[k].start()

    def wait_x_sent(c):
        for k in range(1, nf):
            xs[c, k].wait_send()

    for c in range(2, nch):
        if c == 2:
            wait_x_sent(0)
            send_x(c)
    locate_some(nr // 2, nr)
    for k in range(1, nf):
        sent_g[k].wait_recv()
    c_mom.wait()

    sent_v = {}
    outs = []

    def first_half(c):
        c_x[c].wait()
        for k in range(1, nf):
            xs[c, k].wait_recv()
        cols = slice(c * CHUNK, (c + 1) * CHUNK)
        moment = decay * mom_v[:, cols] + mm(gt[...], xall[c])
        coef = transform(moment, fwd_lh[...], fwd_ll[...], fwd_rh[...], fwd_rl[...])
        own = jnp.where(delta[c, r].astype(F32) == 0.0, coef, 0.0)
        high, low = split(own)
        vt[c, r] = (mm_nt(spot[...], high) + mm_nt(spot[...], low))[:nbc]
        for t in range(1, nr):
            sent_v[c, t] = remote(
                vt.at[c, r], vt.at[c, r], v_s.at[c, t], v_r.at[c, t], lax.rem(r + t, nr), f
            )
            sent_v[c, t].start()
        new_v[:, cols] = moment - transform(
            own, inv_lh[...], inv_ll[...], inv_rh[...], inv_rl[...]
        )
        copy = pltpu.make_async_copy(new_v.at[:, cols], new_out.at[0, :, cols], osem.at[0, c])
        copy.start()
        outs.append(copy)

    def second_half(c):
        for t in range(1, nr):
            sent_v[c, t].wait_recv()
        cols = slice(c * CHUNK, (c + 1) * CHUNK)

        def add_group(g, total):
            first = pl.multiple_of(g * GROUP, GROUP)
            high, low = split(vt[c, pl.ds(first, GROUP)].reshape(GROUP * nbc, rows))
            both = mm_nt(eye[...], jnp.concatenate([high, low], axis=0)).astype(BF)
            for i in range(GROUP):
                value = mm(both, wide8[i])
                total = total + jnp.where(delta[c, first + i].astype(F32) == 0.0, value, 0.0)
            return total

        total = jnp.zeros((rows, CHUNK), F32)
        if nr == GROUP:
            total = add_group(0, total)
        else:
            total = lax.fori_loop(0, nr // GROUP, add_group, total)
        upd_v[:, cols] = transform(total, inv_lh[...], inv_ll[...], inv_rh[...], inv_rl[...])
        copy = pltpu.make_async_copy(upd_v.at[:, cols], upd_out.at[:, cols], osem.at[1, c])
        copy.start()
        outs.append(copy)

    for c in range(nch):
        first_half(c)
        if c + 3 < nch:
            wait_x_sent(c + 1)
            send_x(c + 3)
        if c > 0:
            second_half(c - 1)
    second_half(nch - 1)

    for c in range(max(nch - 2, 0), nch):
        wait_x_sent(c)
    for k in range(1, nf):
        for t in range(1, 4):
            stage2[k, t].wait_send()
        stage3[k].wait_send()
        sent_g[k].wait_send()
    for t in range(1, nr):
        sent_pos[t].wait_send()
        for c in range(nch):
            sent_v[c, t].wait_send()
    for copy in outs:
        copy.wait()


def shards(nf, nr, tokens, weight, cotangent, momentum, chosen):
    td = tokens.shape[0]
    rows, dc = weight.shape
    nch = dc // CHUNK
    nbc = CHUNK // SPAN
    side = 4 * SPAN
    dma = pltpu.SemaphoreType.DMA
    vm = pltpu.VMEM
    new, update = pl.pallas_call(
        functools.partial(kernel, nf, nr),
        out_shape=(
            jax.ShapeDtypeStruct((1, rows, dc), F32),
            jax.ShapeDtypeStruct((rows, dc), F32),
        ),
        in_specs=[pl.BlockSpec(memory_space=pltpu.HBM)] * 5,
        out_specs=(pl.BlockSpec(memory_space=pl.ANY), pl.BlockSpec(memory_space=pl.ANY)),
        scratch_shapes=[
            vm(tokens.shape, BF),
            vm(weight.shape, BF),
            vm((nf, 2, rows, dc // 2), BF),
            vm((rows, td), BF),
            vm((rows, dc), F32),
            vm((nch, nf * td, CHUNK), BF),
            vm((rows, nf * td), BF),
            vm((nr,) + chosen.shape[1:], jnp.int32),
            vm((nch, nr, rows, CHUNK), BF),
            vm((nch, nr, nbc, rows), F32),
            vm((rows, dc), F32),
            vm((rows, dc), F32),
            vm((rows, rows), BF), vm((rows, rows), BF), vm((side, side), BF), vm((side, side), BF),
            vm((rows, rows), BF), vm((rows, rows), BF), vm((side, side), BF), vm((side, side), BF),
            vm((rows, rows), BF), vm((2 * nbc, CHUNK), BF), vm((GROUP, 2 * GROUP * nbc, CHUNK), BF),
            dma((nf,)), dma((nf,)),
            dma((nf, 4)), dma((nf, 4)),
            dma((nf,)), dma((nf,)),
            dma((nf, nch)), dma((nf, nch)),
            dma((nf,)), dma((nf,)),
            dma((nr,)), dma((nr,)),
            dma((nch, nr)), dma((nch, nr)),
            dma((5,)), dma((nch,)), dma((2, nch)),
        ],
        compiler_params=pltpu.CompilerParams(
            collective_id=0, has_side_effects=True, vmem_limit_bytes=60 * 1024 * 1024
        ),
    )(tokens, weight, cotangent.T, momentum, chosen)
    return new, update


def solution(mesh):
    return jax.shard_map(
        functools.partial(shards, mesh.shape["fsdp"], mesh.shape["replica"]),
        mesh=mesh,
        in_specs=(
            P(("replica", "fsdp"), None),
            P(None, "fsdp"),
            P(("replica", "fsdp"), None),
            P("replica", None, "fsdp"),
            P("replica", None, "fsdp", None),
        ),
        out_specs=(P("replica", None, "fsdp"), P(None, "fsdp")),
        check_vma=False,
    )
```
